512 devices in a mesh: seq: 128 (over x_lo, y, z), ch: 4 (over x_hi, core).
Axes of the slice: x: 4 (x_hi: 2, x_lo: 2; x = x_hi * 2 + x_lo), y: 4, z: 16, core: 2. Of those that a mesh axis runs over, the one named last changes fastest.
Arguments:
- query_proj: float32 [64, 131072], P('ch', 'seq'), may hold values from -6 to 6
- key_proj: float32 [64, 131072], P('ch', 'seq'), may hold values from -6 to 6
- value_proj: float32 [64, 131072], P('ch', 'seq'), may hold values from -6 to 6
- filter_taps: float32 [64, 131072], P('ch', 'seq'), may hold values from -6 to 6
- out_cotangent: float32 [64, 131072], P('ch', 'seq'), may hold values from -6 to 6
Outputs:
- hyena_out: float32 [64, 131072], P('ch', 'seq')
- query_grad: float32 [64, 131072], P('ch', 'seq')
- key_grad: float32 [64, 131072], P('ch', 'seq')
- value_grad: float32 [64, 131072], P('ch', 'seq')
- filter_grad: float32 [64, 131072], P('ch', 'seq')
The draws below stay inside these ranges and needn't reach their ends.
All inputs are finite; a program needn't handle non-finite values.
Results may differ from the reference program's by a relative error of at most 0.000098.
Values sent between devices are 32-bit elements; how exact they have to be, the bound alone decides.
A program may use at most 64 MiB of HBM per device.

```python
import jax
import jax.numpy as jnp

SEQ = 131072
CH = 64


def steps_of(key, shape, shards, low, high):
    gain = 1.0
    for axis_at, shards_of in shards:
        steps = jax.random.uniform(jax.random.fold_in(jax.random.fold_in(key, 6), axis_at), (shards_of,), jnp.float32, low / len(shards), high / len(shards))
        gain = gain * jnp.repeat(jnp.exp(steps), shape[axis_at] // shards_of).reshape((-1,) + (1,) * (len(shape) - 1 - axis_at))
    return gain


def bell_draw(rng, dims, deviation, limit, split=(), held_as=jnp.bfloat16):
    array = deviation * jax.random.normal(rng, dims, jnp.float32)
    if split:
        array = array * steps_of(rng, dims, split, -0.22, 0.18)
    return jnp.clip(array, -limit, limit).astype(held_as)


def setup_inputs(seed: int = 0) -> dict:
    streams_of = jax.random.split(jax.random.key(seed), 6)
    return {
        "query_proj": bell_draw(streams_of[0], (CH, SEQ), 1.0, 6.0, ((0, 4), (1, 128)), jnp.float32),
        "key_proj": bell_draw(streams_of[1], (CH, SEQ), 1.0, 6.0, ((0, 4), (1, 128)), jnp.float32),
        "value_proj": bell_draw(streams_of[2], (CH, SEQ), 1.0, 6.0, ((0, 4), (1, 128)), jnp.float32),
        "filter_taps": bell_draw(streams_of[3], (CH, SEQ), 1.0, 6.0, ((0, 4), (1, 128)), jnp.float32),
        "out_cotangent": bell_draw(streams_of[4], (CH, SEQ), 1.0, 6.0, ((0, 4), (1, 128)), jnp.float32),
    }


def reference(query_proj, key_proj, value_proj, filter_taps, out_cotangent):
    full_len = 2 * SEQ
    factor = SEQ ** -0.5
    gated = key_proj * value_proj
    weighted = out_cotangent * query_proj
    gated_spec = jnp.fft.rfft(gated, n=full_len, axis=1)
    filter_spec = jnp.fft.rfft(filter_taps, n=full_len, axis=1)
    weighted_spec = jnp.fft.rfft(weighted, n=full_len, axis=1)
    mixed = jnp.fft.irfft(filter_spec * gated_spec, n=full_len, axis=1)[:, :SEQ] * factor
    gated_grad = jnp.fft.irfft(jnp.conj(filter_spec) * weighted_spec, n=full_len, axis=1)[:, :SEQ] * factor
    filter_grad = jnp.fft.irfft(jnp.conj(gated_spec) * weighted_spec, n=full_len, axis=1)[:, :SEQ] * factor
    mixed = mixed.astype(query_proj.dtype)
    gated_grad = gated_grad.astype(query_proj.dtype)
    filter_grad = filter_grad.astype(query_proj.dtype)
    return (query_proj * mixed, out_cotangent * mixed, gated_grad * value_proj, gated_grad * key_proj, filter_grad)
```

```python
import math

import jax
import jax.numpy as jnp
import numpy as np
from jax import lax
from jax.experimental import pallas as pl
from jax.experimental.pallas import tpu as pltpu
from jax.sharding import PartitionSpec as P

MESH = pl.DeviceIdType.MESH
LANES = 128
ROWS = 8
ITEMS = 3


def split_np(matrix):
    high = matrix.astype(jnp.bfloat16)
    low = (matrix - high.astype(np.float64)).astype(jnp.bfloat16)
    return high, low


def tables(run):
    k1 = np.arange(run)[:, None]
    n1 = np.arange(run)[None, :]
    first = ((2 * k1 + 1) * n1 % (4 * run)) * (2.0 * math.pi / (4 * run))
    first = np.concatenate([np.cos(first), -np.sin(first)], axis=0)
    n2 = np.arange(LANES)[None, :]
    turn = ((2 * k1 + 1) * n2) * (2.0 * math.pi / (4 * run * LANES))
    square = (np.arange(LANES)[:, None] * n2 % LANES) * (2.0 * math.pi / LANES)
    cos, sin = np.cos(square), np.sin(square)
    second = np.block([[cos, -sin], [sin, cos]])
    return (
        *split_np(first),
        np.cos(turn).astype(np.float32),
        (-np.sin(turn)).astype(np.float32),
        *split_np(second),
        *split_np(second.T),
        *split_np(first.T),
    )


def split(value):
    high = value.astype(jnp.bfloat16)
    low = (value - high.astype(jnp.float32)).astype(jnp.bfloat16)
    return high, low


def dot(left, right):
    return jnp.dot(left, right, preferred_element_type=jnp.float32)


def dot3(left, right):
    return dot(left[0], right[0]) + (dot(left[0], right[1]) + dot(left[1], right[0]))


def kernel(
    zs,
    bs,
    scale,
    q_hbm,
    k_hbm,
    v_hbm,
    f_hbm,
    o_hbm,
    *rest,
):
    table_hbm = rest[:10]
    out_refs = rest[10:15]
    (
        q_ref,
        k_ref,
        v_ref,
        f_ref,
        o_ref,
        *table_refs,
    ) = rest[15:30]
    (
        a_send,
        a_recv,
        b_send,
        b_recv,
        c_send,
        c_recv,
        d_send,
        d_recv,
        in_sem,
        send_sem,
        recv_sem,
    ) = rest[30:]
    run = zs * ROWS
    part = run // bs
    me = lax.axis_index("seq")
    block = me // zs
    lane = me % zs

    def z_peer(step):
        return lax.rem(lane + step, zs)

    def b_peer(step):
        return lax.rem(block + step, bs)

    barrier = pltpu.get_barrier_semaphore()

    @pl.loop(1, zs)
    def _(step):
        pl.semaphore_signal(
            barrier, inc=1, device_id={"seq": block * zs + z_peer(step)}, device_id_type=MESH
        )

    @pl.loop(1, bs)
    def _(step):
        pl.semaphore_signal(
            barrier, inc=1, device_id={"seq": b_peer(step) * zs + lane}, device_id_type=MESH
        )

    loads = [
        pltpu.make_async_copy(src, dst, in_sem.at[at])
        for at, (src, dst) in enumerate(
            zip(
                (k_hbm, v_hbm, f_hbm, o_hbm, q_hbm) + tuple(table_hbm),
                (k_ref, v_ref, f_ref, o_ref, q_ref) + tuple(table_refs),
            )
        )
    ]
    for load in loads:
        load.start()

    def fill(item, value):
        for row in range(ROWS):
            a_send[item, :, row, :] = value[:, row * LANES : (row + 1) * LANES]
        a_recv[item, lane] = a_send[item, lane]

    def spread_z(phase, item, source, target):
        @pl.loop(1, zs)
        def _(step):
            peer = z_peer(step)
            pltpu.make_async_remote_copy(
                src_ref=source.at[item, peer],
                dst_ref=target.at[item, lane],
                send_sem=send_sem.at[phase, item],
                recv_sem=recv_sem.at[phase, item],
                device_id={"seq": block * zs + peer},
                device_id_type=MESH,
            ).start()

    def spread_b(phase, item, source, target):
        @pl.loop(1, bs)
        def _(step):
            peer = b_peer(step)
            pltpu.make_async_remote_copy(
                src_ref=source.at[item, peer],
                dst_ref=target.at[item, block],
                send_sem=send_sem.at[phase, item],
                recv_sem=recv_sem.at[phase, item],
                device_id={"seq": peer * zs + lane},
                device_id_type=MESH,
            ).start()

    def await_all(sems, phase, item, buffer, count):
        whole = buffer.at[item, pl.ds(0, count - 1)]
        pltpu.make_async_copy(whole, whole, sems.at[phase, item]).wait()

    loads[0].wait()
    loads[1].wait()
    fill(0, k_ref[...] * v_ref[...])
    loads[2].wait()
    fill(1, f_ref[...])
    loads[3].wait()
    loads[4].wait()
    fill(2, o_ref[...] * q_ref[...])
    pl.semaphore_wait(barrier, zs - 1 + bs - 1)
    for item in range(ITEMS):
        spread_z(0, item, a_send, a_recv)
    for load in loads[5:]:
        load.wait()
    first = (table_refs[0], table_refs[1])
    turn_real, turn_imag = table_refs[2], table_refs[3]
    second = (table_refs[4], table_refs[5])
    second_back = (table_refs[6], table_refs[7])
    first_back = (table_refs[8], table_refs[9])

    def pair(refs):
        return refs[0][...], refs[1][...]

    def forward(item):
        await_all(recv_sem, 0, item, a_recv, zs)
        rows = a_recv[item].reshape(run, LANES)
        sums = dot3(pair(first), split(rows))
        real, imag = sums[:run], sums[run:]
        cos, sin = turn_real[...], turn_imag[...]
        turned = jnp.concatenate([real * cos - imag * sin, real * sin + imag * cos], axis=1)
        bins = dot3(split(turned), pair(second))
        b_send[item, :, 0] = bins[:, :LANES].reshape(bs, part, LANES)
        b_send[item, :, 1] = bins[:, LANES:].reshape(bs, part, LANES)
        b_recv[item, block] = b_send[item, block]
        spread_b(1, item, b_send, b_recv)

    sign = 1.0 - 2.0 * (lax.broadcasted_iota(jnp.int32, (part, LANES), 0) % 2).astype(jnp.float32)

    def spectrum(item, at):
        return b_recv[item, at, 0], b_recv[item, at, 1]

    def finish(item, sums, step, factor):
        for at in range(bs):
            real, imag = sums[at]
            other = at + step
            if 0 <= other < bs:
                over_real, over_imag = sums[other]
                real = real - factor * over_imag
                imag = imag + factor * over_real
            c_send[item, at, 0] = real
            c_send[item, at, 1] = imag
        c_recv[item, block] = c_send[item, block]
        spread_b(2, item, c_send, c_recv)

    def convolve(item, left, right):
        sums = []
        for at in range(bs):
            real = imag = None
            for of in range(at + 1):
                lr, li = spectrum(left, at - of)
                rr, ri = spectrum(right, of)
                pr, pi = lr * rr - li * ri, lr * ri + li * rr
                real, imag = (pr, pi) if real is None else (real + pr, imag + pi)
            sums.append((real, imag))
        finish(item, sums, -1, sign)

    def correlate(item, left, right):
        sums = []
        for at in range(bs):
            real = imag = None
            for of in range(bs - at):
                lr, li = spectrum(left, of)
                rr, ri = spectrum(right, at + of)
                pr, pi = lr * rr + li * ri, lr * ri - li * rr
                real, imag = (pr, pi) if real is None else (real + pr, imag + pi)
            sums.append((real, imag))
        finish(item, sums, 1, -sign)

    def inverse(item):
        await_all(recv_sem, 2, item, c_recv, bs)
        bins = jnp.concatenate(
            [c_recv[item, :, 0].reshape(run, LANES), c_recv[item, :, 1].reshape(run, LANES)], axis=1
        )
        sums = dot3(split(bins), pair(second_back))
        real, imag = sums[:, :LANES], sums[:, LANES:]
        cos, sin = turn_real[...], turn_imag[...]
        turned = jnp.concatenate([real * cos + imag * sin, imag * cos - real * sin], axis=0)
        rows = dot3(pair(first_back), split(turned)) * scale
        d_send[item] = rows.reshape(zs, ROWS, LANES)
        d_recv[item, lane] = d_send[item, lane]
        spread_z(3, item, d_send, d_recv)

    forward(0)
    forward(1)
    forward(2)
    await_all(recv_sem, 1, 0, b_recv, bs)
    await_all(recv_sem, 1, 1, b_recv, bs)
    convolve(0, 1, 0)
    await_all(recv_sem, 1, 2, b_recv, bs)
    correlate(1, 1, 2)
    correlate(2, 0, 2)
    inverse(0)
    inverse(1)
    inverse(2)

    for item in range(ITEMS):
        await_all(send_sem, 0, item, a_send, zs)
        await_all(send_sem, 1, item, b_send, bs)
        await_all(send_sem, 2, item, c_send, bs)
    await_all(recv_sem, 3, 0, d_recv, zs)
    for row in range(ROWS):
        here = slice(row * LANES, (row + 1) * LANES)
        mixed = d_recv[0, :, row, :]
        out_refs[0][:, here] = q_ref[:, here] * mixed
        out_refs[1][:, here] = o_ref[:, here] * mixed
    await_all(recv_sem, 3, 1, d_recv, zs)
    for row in range(ROWS):
        here = slice(row * LANES, (row + 1) * LANES)
        gated_grad = d_recv[1, :, row, :]
        out_refs[2][:, here] = gated_grad * v_ref[:, here]
        out_refs[3][:, here] = gated_grad * k_ref[:, here]
    await_all(recv_sem, 3, 2, d_recv, zs)
    for row in range(ROWS):
        out_refs[4][:, row * LANES : (row + 1) * LANES] = d_recv[2, :, row, :]
    for item in range(ITEMS):
        await_all(send_sem, 3, item, d_send, zs)


def per_device(query_proj, key_proj, value_proj, filter_taps, out_cotangent):
    devices = lax.axis_size("seq")
    channels, tokens = filter_taps.shape
    zs = channels
    bs = devices // zs
    run = zs * ROWS
    part = run // bs
    scale = 1.0 / (run * LANES * math.sqrt(tokens * devices))
    table = tables(run)
    shape = jax.ShapeDtypeStruct((channels, tokens), jnp.float32)
    z_buffer = pltpu.VMEM((ITEMS, zs, ROWS, LANES), jnp.float32)
    b_buffer = pltpu.VMEM((ITEMS, bs, 2, part, LANES), jnp.float32)
    body = lambda *refs: kernel(zs, bs, scale, *refs)
    outs = pl.pallas_call(
        body,
        out_shape=[shape] * 5,
        in_specs=[pl.BlockSpec(memory_space=pl.ANY)] * (5 + len(table)),
        out_specs=[pl.BlockSpec(memory_space=pltpu.VMEM)] * 5,
        scratch_shapes=[
            *[pltpu.VMEM((channels, tokens), jnp.float32) for _ in range(5)],
            *[pltpu.VMEM(entry.shape, entry.dtype) for entry in table],
            z_buffer,
            z_buffer,
            b_buffer,
            b_buffer,
            b_buffer,
            b_buffer,
            z_buffer,
            z_buffer,
            pltpu.SemaphoreType.DMA((5 + len(table),)),
            pltpu.SemaphoreType.DMA((4, ITEMS)),
            pltpu.SemaphoreType.DMA((4, ITEMS)),
        ],
        compiler_params=pltpu.CompilerParams(
            collective_id=0, has_side_effects=True, vmem_limit_bytes=32 * 1024 * 1024
        ),
    )(
        query_proj,
        key_proj,
        value_proj,
        filter_taps,
        out_cotangent,
        *[jnp.asarray(entry) for entry in table],
    )
    return tuple(outs)


def solution(mesh):
    placed = (P("ch", "seq"),) * 5
    return jax.shard_map(
        per_device, mesh=mesh, in_specs=placed, out_specs=placed, check_vma=False
    )
```

```python
import math

import jax
import jax.numpy as jnp
import numpy as np
from jax import lax
from jax.experimental import pallas as pl
from jax.experimental.pallas import tpu as pltpu
from jax.sharding import PartitionSpec as P

MESH = pl.DeviceIdType.MESH
LANES = 128
ROWS = 8
ITEMS = 3


def split_np(matrix):
    high = matrix.astype(jnp.bfloat16)
    low = (matrix - high.astype(np.float64)).astype(jnp.bfloat16)
    return high, low


def tables(run):
    k1 = np.arange(run)[:, None]
    n1 = np.arange(run)[None, :]
    first = ((2 * k1 + 1) * n1 % (4 * run)) * (2.0 * math.pi / (4 * run))
    first = np.concatenate([np.cos(first), -np.sin(first)], axis=0)
    n2 = np.arange(LANES)[None, :]
    turn = ((2 * k1 + 1) * n2) * (2.0 * math.pi / (4 * run * LANES))
    square = (np.arange(LANES)[:, None] * n2 % LANES) * (2.0 * math.pi / LANES)
    cos, sin = np.cos(square), np.sin(square)
    second = np.block([[cos, -sin], [sin, cos]])
    return (
        *split_np(first),
        np.cos(turn).astype(np.float32),
        (-np.sin(turn)).astype(np.float32),
        *split_np(second),
        *split_np(second.T),
        *split_np(first.T),
    )


def split(value):
    high = value.astype(jnp.bfloat16)
    low = (value - high.astype(jnp.float32)).astype(jnp.bfloat16)
    return high, low


def dot(left, right):
    return jnp.dot(left, right, preferred_element_type=jnp.float32)


def dot3(left, right):
    return dot(left[0], right[0]) + (dot(left[0], right[1]) + dot(left[1], right[0]))


def z_order(count):
    near = [step for half in range((count - 1) // 2, 0, -1) for step in (half, count - half)]
    return ([count // 2] if count % 2 == 0 else []) + near


def b_order(count):
    wide = count // 2
    steps = [(dx, dy) for dx in range(2) for dy in range(wide) if dx or dy]
    return sorted(steps, key=lambda step: -(step[0] + min(step[1], wide - step[1])))


def kernel(
    zs,
    bs,
    scale,
    q_hbm,
    k_hbm,
    v_hbm,
    f_hbm,
    o_hbm,
    *rest,
):
    table_hbm = rest[:10]
    out_hbm = rest[10]
    (
        q_ref,
        k_ref,
        v_ref,
        f_ref,
        o_ref,
        *table_refs,
    ) = rest[11:26]
    (
        a_send,
        a_recv,
        b_send,
        b_recv,
        c_send,
        c_recv,
        d_send,
        d_recv,
        out_ref,
        in_sem,
        out_sem,
        send_sem,
        recv_sem,
    ) = rest[26:]
    run = zs * ROWS
    part = run // bs
    me = lax.axis_index("seq")
    block = me // zs
    lane = me % zs

    def z_peer(step):
        return lax.rem(lane + step, zs)

    def b_peer(step):
        wide = bs // 2
        across = lax.rem(lax.div(block, wide) + step[0], 2)
        return across * wide + lax.rem(lax.rem(block, wide) + step[1], wide)

    barrier = pltpu.get_barrier_semaphore()
    for step in z_order(zs):
        pl.semaphore_signal(
            barrier, inc=1, device_id={"seq": block * zs + z_peer(step)}, device_id_type=MESH
        )
    for step in b_order(bs):
        pl.semaphore_signal(
            barrier, inc=1, device_id={"seq": b_peer(step) * zs + lane}, device_id_type=MESH
        )

    loads = [
        pltpu.make_async_copy(src, dst, in_sem.at[at])
        for at, (src, dst) in enumerate(
            zip(
                (k_hbm, v_hbm, f_hbm, o_hbm, q_hbm) + tuple(table_hbm),
                (k_ref, v_ref, f_ref, o_ref, q_ref) + tuple(table_refs),
            )
        )
    ]
    for load in loads:
        load.start()

    def fill(item, value):
        for row in range(ROWS):
            a_send[:, item, row, :] = value[:, row * LANES : (row + 1) * LANES]
        a_recv[lane, item] = a_send[lane, item]

    def spread_a(group, items):
        for step in z_order(zs):
            peer = z_peer(step)
            pltpu.make_async_remote_copy(
                src_ref=a_send.at[peer, items],
                dst_ref=a_recv.at[lane, items],
                send_sem=send_sem.at[0, group],
                recv_sem=recv_sem.at[0, group],
                device_id={"seq": block * zs + peer},
                device_id_type=MESH,
            ).start()

    def await_a(sems, group, items, buffer):
        whole = buffer.at[pl.ds(0, zs - 1), items]
        pltpu.make_async_copy(whole, whole, sems.at[0, group]).wait()

    def spread_z(phase, item, source, target):
        for step in z_order(zs):
            peer = z_peer(step)
            pltpu.make_async_remote_copy(
                src_ref=source.at[item, peer],
                dst_ref=target.at[item, lane],
                send_sem=send_sem.at[phase, item],
                recv_sem=recv_sem.at[phase, item],
                device_id={"seq": block * zs + peer},
                device_id_type=MESH,
            ).start()

    def spread_b(phase, item, source, target):
        for step in b_order(bs):
            peer = b_peer(step)
            pltpu.make_async_remote_copy(
                src_ref=source.at[item, peer],
                dst_ref=target.at[item, block],
                send_sem=send_sem.at[phase, item],
                recv_sem=recv_sem.at[phase, item],
                device_id={"seq": peer * zs + lane},
                device_id_type=MESH,
            ).start()

    def await_all(sems, phase, item, buffer, count):
        whole = buffer.at[item, pl.ds(0, count - 1)]
        pltpu.make_async_copy(whole, whole, sems.at[phase, item]).wait()

    groups = (pl.ds(0, 2), pl.ds(2, 1))
    loads[0].wait()
    loads[1].wait()
    fill(0, k_ref[...] * v_ref[...])
    loads[2].wait()
    fill(1, f_ref[...])
    loads[3].wait()
    loads[4].wait()
    fill(2, o_ref[...] * q_ref[...])
    pl.semaphore_wait(barrier, zs - 1 + bs - 1)
    for group, items in enumerate(groups):
        spread_a(group, items)
    for load in loads[5:]:
        load.wait()
    first = (table_refs[0], table_refs[1])
    turn_real, turn_imag = table_refs[2], table_refs[3]
    second = (table_refs[4], table_refs[5])
    second_back = (table_refs[6], table_refs[7])
    first_back = (table_refs[8], table_refs[9])

    def pair(refs):
        return refs[0][...], refs[1][...]

    def forward(item):
        rows = a_recv[:, item].reshape(run, LANES)
        sums = dot3(pair(first), split(rows))
        real, imag = sums[:run], sums[run:]
        cos, sin = turn_real[...], turn_imag[...]
        turned = jnp.concatenate([real * cos - imag * sin, real * sin + imag * cos], axis=1)
        bins = dot3(split(turned), pair(second))
        b_send[item, :, 0] = bins[:, :LANES].reshape(bs, part, LANES)
        b_send[item, :, 1] = bins[:, LANES:].reshape(bs, part, LANES)
        b_recv[item, block] = b_send[item, block]
        spread_b(1, item, b_send, b_recv)

    sign = 1.0 - 2.0 * (lax.broadcasted_iota(jnp.int32, (part, LANES), 0) % 2).astype(jnp.float32)

    def spectrum(item, at):
        return b_recv[item, at, 0], b_recv[item, at, 1]

    def finish(item, sums, step, factor):
        for at in range(bs):
            real, imag = sums[at]
            other = at + step
            if 0 <= other < bs:
                over_real, over_imag = sums[other]
                real = real - factor * over_imag
                imag = imag + factor * over_real
            c_send[item, at, 0] = real
            c_send[item, at, 1] = imag
        c_recv[item, block] = c_send[item, block]
        spread_b(2, item, c_send, c_recv)

    def convolve(item, left, right):
        sums = []
        for at in range(bs):
            real = imag = None
            for of in range(at + 1):
                lr, li = spectrum(left, at - of)
                rr, ri = spectrum(right, of)
                pr, pi = lr * rr - li * ri, lr * ri + li * rr
                real, imag = (pr, pi) if real is None else (real + pr, imag + pi)
            sums.append((real, imag))
        finish(item, sums, -1, sign)

    def correlate(item, left, right):
        sums = []
        for at in range(bs):
            real = imag = None
            for of in range(bs - at):
                lr, li = spectrum(left, of)
                rr, ri = spectrum(right, at + of)
                pr, pi = lr * rr + li * ri, lr * ri - li * rr
                real, imag = (pr, pi) if real is None else (real + pr, imag + pi)
            sums.append((real, imag))
        finish(item, sums, 1, -sign)

    def inverse(item):
        await_all(recv_sem, 2, item, c_recv, bs)
        bins = jnp.concatenate(
            [c_recv[item, :, 0].reshape(run, LANES), c_recv[item, :, 1].reshape(run, LANES)], axis=1
        )
        sums = dot3(split(bins), pair(second_back))
        real, imag = sums[:, :LANES], sums[:, LANES:]
        cos, sin = turn_real[...], turn_imag[...]
        turned = jnp.concatenate([real * cos + imag * sin, imag * cos - real * sin], axis=0)
        rows = dot3(pair(first_back), split(turned)) * scale
        d_send[item] = rows.reshape(zs, ROWS, LANES)
        d_recv[item, lane] = d_send[item, lane]
        spread_z(3, item, d_send, d_recv)

    await_a(recv_sem, 0, groups[0], a_recv)
    forward(0)
    forward(1)
    await_a(recv_sem, 1, groups[1], a_recv)
    forward(2)
    await_all(recv_sem, 1, 0, b_recv, bs)
    await_all(recv_sem, 1, 1, b_recv, bs)
    convolve(0, 1, 0)
    await_all(recv_sem, 1, 2, b_recv, bs)
    correlate(1, 1, 2)
    correlate(2, 0, 2)
    inverse(0)
    inverse(1)
    inverse(2)

    stores = []

    def store(item, at, count):
        rows = pl.ds(at, count)
        copy = pltpu.make_async_copy(out_ref.at[rows], out_hbm.at[rows], out_sem.at[item])
        copy.start()
        stores.append(copy)

    for item in range(ITEMS):
        await_all(send_sem, 1, item, b_send, bs)
        await_all(send_sem, 2, item, c_send, bs)
    for group, items in enumerate(groups):
        await_a(send_sem, group, items, a_send)
    await_all(recv_sem, 3, 0, d_recv, zs)
    for row in range(ROWS):
        here = slice(row * LANES, (row + 1) * LANES)
        mixed = d_recv[0, :, row, :]
        out_ref[0, :, here] = q_ref[:, here] * mixed
        out_ref[1, :, here] = o_ref[:, here] * mixed
    store(0, 0, 2)
    await_all(recv_sem, 3, 1, d_recv, zs)
    for row in range(ROWS):
        here = slice(row * LANES, (row + 1) * LANES)
        gated_grad = d_recv[1, :, row, :]
        out_ref[2, :, here] = gated_grad * v_ref[:, here]
        out_ref[3, :, here] = gated_grad * k_ref[:, here]
    store(1, 2, 2)
    await_all(recv_sem, 3, 2, d_recv, zs)
    for row in range(ROWS):
        out_ref[4, :, row * LANES : (row + 1) * LANES] = d_recv[2, :, row, :]
    store(2, 4, 1)
    for item in range(ITEMS):
        await_all(send_sem, 3, item, d_send, zs)
    for copy in stores:
        copy.wait()


def per_device(query_proj, key_proj, value_proj, filter_taps, out_cotangent):
    devices = lax.axis_size("seq")
    channels, tokens = filter_taps.shape
    zs = channels
    bs = devices // zs
    run = zs * ROWS
    part = run // bs
    scale = 1.0 / (run * LANES * math.sqrt(tokens * devices))
    table = tables(run)
    a_buffer = pltpu.VMEM((zs, ITEMS, ROWS, LANES), jnp.float32)
    z_buffer = pltpu.VMEM((ITEMS, zs, ROWS, LANES), jnp.float32)
    b_buffer = pltpu.VMEM((ITEMS, bs, 2, part, LANES), jnp.float32)
    body = lambda *refs: kernel(zs, bs, scale, *refs)
    outs = pl.pallas_call(
        body,
        out_shape=jax.ShapeDtypeStruct((5, channels, tokens), jnp.float32),
        in_specs=[pl.BlockSpec(memory_space=pl.ANY)] * (5 + len(table)),
        out_specs=pl.BlockSpec(memory_space=pl.ANY),
        scratch_shapes=[
            *[pltpu.VMEM((channels, tokens), jnp.float32) for _ in range(5)],
            *[pltpu.VMEM(entry.shape, entry.dtype) for entry in table],
            a_buffer,
            a_buffer,
            b_buffer,
            b_buffer,
            b_buffer,
            b_buffer,
            z_buffer,
            z_buffer,
            pltpu.VMEM((5, channels, tokens), jnp.float32),
            pltpu.SemaphoreType.DMA((5 + len(table),)),
            pltpu.SemaphoreType.DMA((3,)),
            pltpu.SemaphoreType.DMA((4, ITEMS)),
            pltpu.SemaphoreType.DMA((4, ITEMS)),
        ],
        compiler_params=pltpu.CompilerParams(
            collective_id=0, has_side_effects=True, vmem_limit_bytes=60 * 1024 * 1024
        ),
    )(
        query_proj,
        key_proj,
        value_proj,
        filter_taps,
        out_cotangent,
        *[jnp.asarray(entry) for entry in table],
    )
    return tuple(outs[at] for at in range(5))


def solution(mesh):
    placed = (P("ch", "seq"),) * 5
    return jax.shard_map(
        per_device, mesh=mesh, in_specs=placed, out_specs=placed, check_vma=False
    )
```

```python
import math

import jax
import jax.numpy as jnp
import numpy as np
from jax import lax
from jax.experimental import pallas as pl
from jax.experimental.pallas import tpu as pltpu
from jax.sharding import PartitionSpec as P

MESH = pl.DeviceIdType.MESH
LANES = 128
ROWS = 8
ITEMS = 3


def split_np(matrix):
    high = matrix.astype(jnp.bfloat16)
    low = (matrix - high.astype(np.float64)).astype(jnp.bfloat16)
    return high, low


def tables(run):
    k1 = np.arange(run)[:, None]
    n1 = np.arange(run)[None, :]
    first = ((2 * k1 + 1) * n1 % (4 * run)) * (2.0 * math.pi / (4 * run))
    first = np.concatenate([np.cos(first), -np.sin(first)], axis=0)
    n2 = np.arange(LANES)[None, :]
    turn = ((2 * k1 + 1) * n2) * (2.0 * math.pi / (4 * run * LANES))
    square = (np.arange(LANES)[:, None] * n2 % LANES) * (2.0 * math.pi / LANES)
    cos, sin = np.cos(square), np.sin(square)
    second = np.block([[cos, -sin], [sin, cos]])
    def left(matrix):
        high, low = split_np(matrix)
        return np.concatenate([high, high, low], axis=1)

    def right(matrix):
        high, low = split_np(matrix)
        return np.concatenate([high, high, low], axis=0)

    return (
        left(first),
        np.cos(turn).astype(np.float32),
        (-np.sin(turn)).astype(np.float32),
        right(second),
        right(second.T),
        left(first.T),
    )


def split(value):
    high = value.astype(jnp.bfloat16)
    low = (value - high.astype(jnp.float32)).astype(jnp.bfloat16)
    return high, low


def dot(left, right):
    return jnp.dot(left, right, preferred_element_type=jnp.float32)


def dot_left(table, value):
    high, low = split(value)
    return dot(table, jnp.concatenate([high, low, high], axis=0))


def dot_right(value, table):
    high, low = split(value)
    return dot(jnp.concatenate([high, low, high], axis=1), table)


def z_order(count):
    near = [step for half in range((count - 1) // 2, 0, -1) for step in (half, count - half)]
    return ([count // 2] if count % 2 == 0 else []) + near


def b_order(count):
    wide = count // 2
    steps = [(dx, dy) for dx in range(2) for dy in range(wide) if dx or dy]
    return sorted(steps, key=lambda step: -(step[0] + min(step[1], wide - step[1])))


def kernel(
    zs,
    bs,
    scale,
    q_hbm,
    k_hbm,
    v_hbm,
    f_hbm,
    o_hbm,
    *rest,
):
    table_hbm = rest[:6]
    out_ref = rest[6]
    (
        q_ref,
        k_ref,
        v_ref,
        f_ref,
        o_ref,
        *table_refs,
    ) = rest[7:18]
    (
        a_send,
        a_recv,
        b_send,
        b_recv,
        c_send,
        c_recv,
        d_send,
        d_recv,
        in_sem,
        send_sem,
        recv_sem,
    ) = rest[18:]
    run = zs * ROWS
    part = run // bs
    me = lax.axis_index("seq")
    block = me // zs
    lane = me % zs

    def z_peer(step):
        return lax.rem(lane + step, zs)

    def b_peer(step):
        wide = bs // 2
        across = lax.rem(lax.div(block, wide) + step[0], 2)
        return across * wide + lax.rem(lax.rem(block, wide) + step[1], wide)

    barrier = pltpu.get_barrier_semaphore()
    for step in z_order(zs):
        pl.semaphore_signal(
            barrier, inc=1, device_id={"seq": block * zs + z_peer(step)}, device_id_type=MESH
        )
    for step in b_order(bs):
        pl.semaphore_signal(
            barrier, inc=1, device_id={"seq": b_peer(step) * zs + lane}, device_id_type=MESH
        )

    loads = [
        pltpu.make_async_copy(src, dst, in_sem.at[at])
        for at, (src, dst) in enumerate(
            zip(
                (k_hbm, v_hbm, f_hbm, o_hbm, q_hbm) + tuple(table_hbm),
                (k_ref, v_ref, f_ref, o_ref, q_ref) + tuple(table_refs),
            )
        )
    ]
    for load in loads:
        load.start()

    def fill(item, value):
        for row in range(ROWS):
            a_send[:, item, row, :] = value[:, row * LANES : (row + 1) * LANES]
        a_recv[lane, item] = a_send[lane, item]

    def spread_z(phase, group, items, source, target):
        for step in z_order(zs):
            peer = z_peer(step)
            pltpu.make_async_remote_copy(
                src_ref=source.at[peer, items],
                dst_ref=target.at[lane, items],
                send_sem=send_sem.at[phase, group],
                recv_sem=recv_sem.at[phase, group],
                device_id={"seq": block * zs + peer},
                device_id_type=MESH,
            ).start()

    def await_z(sems, phase, group, items, buffer):
        whole = buffer.at[pl.ds(0, zs - 1), items]
        pltpu.make_async_copy(whole, whole, sems.at[phase, group]).wait()

    def spread_b(phase, item, source, target):
        for step in b_order(bs):
            peer = b_peer(step)
            pltpu.make_async_remote_copy(
                src_ref=source.at[item, peer],
                dst_ref=target.at[item, block],
                send_sem=send_sem.at[phase, item],
                recv_sem=recv_sem.at[phase, item],
                device_id={"seq": peer * zs + lane},
                device_id_type=MESH,
            ).start()

    def spread_c(group, items):
        for step in b_order(bs):
            peer = b_peer(step)
            pltpu.make_async_remote_copy(
                src_ref=c_send.at[peer, items],
                dst_ref=c_recv.at[block, items],
                send_sem=send_sem.at[2, group],
                recv_sem=recv_sem.at[2, group],
                device_id={"seq": peer * zs + lane},
                device_id_type=MESH,
            ).start()

    def await_c(sems, group, items, buffer):
        whole = buffer.at[pl.ds(0, bs - 1), items]
        pltpu.make_async_copy(whole, whole, sems.at[2, group]).wait()

    def await_all(sems, phase, item, buffer, count):
        whole = buffer.at[item, pl.ds(0, count - 1)]
        pltpu.make_async_copy(whole, whole, sems.at[phase, item]).wait()

    groups = (pl.ds(0, 2), pl.ds(2, 1))
    returns = (pl.ds(0, 1), pl.ds(1, 2))
    loads[0].wait()
    loads[1].wait()
    fill(0, k_ref[...] * v_ref[...])
    loads[2].wait()
    fill(1, f_ref[...])
    loads[3].wait()
    loads[4].wait()
    fill(2, o_ref[...] * q_ref[...])
    pl.semaphore_wait(barrier, zs - 1 + bs - 1)
    for group, items in enumerate(groups):
        spread_z(0, group, items, a_send, a_recv)
    for load in loads[5:]:
        load.wait()
    first, turn_real, turn_imag, second, second_back, first_back = table_refs

    def forward(items):
        rows = [a_recv[:, item].reshape(run, LANES) for item in items]
        sums = dot_left(first[...], jnp.concatenate(rows, axis=1))
        cos, sin = turn_real[...], turn_imag[...]
        turned = []
        for at in range(len(items)):
            here = slice(at * LANES, (at + 1) * LANES)
            real, imag = sums[:run, here], sums[run:, here]
            turned.append(
                jnp.concatenate([real * cos - imag * sin, real * sin + imag * cos], axis=1)
            )
        bins = dot_right(jnp.concatenate(turned, axis=0), second[...])
        for at, item in enumerate(items):
            here = slice(at * run, (at + 1) * run)
            b_send[item, :, 0] = bins[here, :LANES].reshape(bs, part, LANES)
            b_send[item, :, 1] = bins[here, LANES:].reshape(bs, part, LANES)
            b_recv[item, block] = b_send[item, block]
            spread_b(1, item, b_send, b_recv)

    sign = 1.0 - 2.0 * (lax.broadcasted_iota(jnp.int32, (part, LANES), 0) % 2).astype(jnp.float32)

    def spectrum(item, at):
        return b_recv[item, at, 0], b_recv[item, at, 1]

    def finish(item, sums, step, factor):
        for at in range(bs):
            real, imag = sums[at]
            other = at + step
            if 0 <= other < bs:
                over_real, over_imag = sums[other]
                real = real - factor * over_imag
                imag = imag + factor * over_real
            c_send[at, item, 0] = real
            c_send[at, item, 1] = imag
        c_recv[block, item] = c_send[block, item]

    def convolve(item, left, right):
        sums = []
        for at in range(bs):
            real = imag = None
            for of in range(at + 1):
                lr, li = spectrum(left, at - of)
                rr, ri = spectrum(right, of)
                pr, pi = lr * rr - li * ri, lr * ri + li * rr
                real, imag = (pr, pi) if real is None else (real + pr, imag + pi)
            sums.append((real, imag))
        finish(item, sums, -1, sign)

    def correlate(item, left, right):
        sums = []
        for at in range(bs):
            real = imag = None
            for of in range(bs - at):
                lr, li = spectrum(left, of)
                rr, ri = spectrum(right, at + of)
                pr, pi = lr * rr + li * ri, lr * ri - li * rr
                real, imag = (pr, pi) if real is None else (real + pr, imag + pi)
            sums.append((real, imag))
        finish(item, sums, 1, -sign)

    def inverse(items):
        bins = [
            jnp.concatenate(
                [c_recv[:, item, half].reshape(run, LANES) for half in range(2)], axis=1
            )
            for item in items
        ]
        sums = dot_right(jnp.concatenate(bins, axis=0), second_back[...])
        cos, sin = turn_real[...], turn_imag[...]
        turned = []
        for at in range(len(items)):
            here = slice(at * run, (at + 1) * run)
            real, imag = sums[here, :LANES], sums[here, LANES:]
            turned.append(
                jnp.concatenate([real * cos + imag * sin, imag * cos - real * sin], axis=0)
            )
        rows = dot_left(first_back[...], jnp.concatenate(turned, axis=1)) * scale
        for at, item in enumerate(items):
            here = slice(at * LANES, (at + 1) * LANES)
            d_send[:, item] = rows[:, here].reshape(zs, ROWS, LANES)
            d_recv[lane, item] = d_send[lane, item]

    await_z(recv_sem, 0, 0, groups[0], a_recv)
    forward((0, 1))
    await_z(recv_sem, 0, 1, groups[1], a_recv)
    forward((2,))
    await_all(recv_sem, 1, 0, b_recv, bs)
    await_all(recv_sem, 1, 1, b_recv, bs)
    convolve(0, 1, 0)
    spread_c(0, returns[0])
    await_all(recv_sem, 1, 2, b_recv, bs)
    correlate(1, 1, 2)
    correlate(2, 0, 2)
    spread_c(1, returns[1])
    await_c(recv_sem, 0, returns[0], c_recv)
    inverse((0,))
    spread_z(3, 0, returns[0], d_send, d_recv)
    await_c(recv_sem, 1, returns[1], c_recv)
    inverse((1, 2))
    spread_z(3, 1, returns[1], d_send, d_recv)

    for item in range(ITEMS):
        await_all(send_sem, 1, item, b_send, bs)
    for group, items in enumerate(returns):
        await_c(send_sem, group, items, c_send)
    for group, items in enumerate(groups):
        await_z(send_sem, 0, group, items, a_send)
    await_z(recv_sem, 3, 0, returns[0], d_recv)
    for row in range(ROWS):
        here = slice(row * LANES, (row + 1) * LANES)
        mixed = d_recv[:, 0, row, :]
        out_ref[0, :, here] = q_ref[:, here] * mixed
        out_ref[1, :, here] = o_ref[:, here] * mixed
    await_z(recv_sem, 3, 1, returns[1], d_recv)
    for row in range(ROWS):
        here = slice(row * LANES, (row + 1) * LANES)
        gated_grad = d_recv[:, 1, row, :]
        out_ref[2, :, here] = gated_grad * v_ref[:, here]
        out_ref[3, :, here] = gated_grad * k_ref[:, here]
    for row in range(ROWS):
        out_ref[4, :, row * LANES : (row + 1) * LANES] = d_recv[:, 2, row, :]
    for group, items in enumerate(returns):
        await_z(send_sem, 3, group, items, d_send)


def per_device(query_proj, key_proj, value_proj, filter_taps, out_cotangent):
    devices = lax.axis_size("seq")
    channels, tokens = filter_taps.shape
    zs = channels
    bs = devices // zs
    run = zs * ROWS
    part = run // bs
    scale = 1.0 / (run * LANES * math.sqrt(tokens * devices))
    table = tables(run)
    z_buffer = pltpu.VMEM((zs, ITEMS, ROWS, LANES), jnp.float32)
    c_buffer = pltpu.VMEM((bs, ITEMS, 2, part, LANES), jnp.float32)
    b_buffer = pltpu.VMEM((ITEMS, bs, 2, part, LANES), jnp.float32)
    body = lambda *refs: kernel(zs, bs, scale, *refs)
    outs = pl.pallas_call(
        body,
        out_shape=pltpu.VMEM((5, channels, tokens), jnp.float32),
        in_specs=[pl.BlockSpec(memory_space=pl.ANY)] * (5 + len(table)),
        out_specs=pl.BlockSpec(memory_space=pltpu.VMEM),
        scratch_shapes=[
            *[pltpu.VMEM((channels, tokens), jnp.float32) for _ in range(5)],
            *[pltpu.VMEM(entry.shape, entry.dtype) for entry in table],
            z_buffer,
            z_buffer,
            b_buffer,
            b_buffer,
            c_buffer,
            c_buffer,
            z_buffer,
            z_buffer,
            pltpu.SemaphoreType.DMA((5 + len(table),)),
            pltpu.SemaphoreType.DMA((4, ITEMS)),
            pltpu.SemaphoreType.DMA((4, ITEMS)),
        ],
        compiler_params=pltpu.CompilerParams(
            collective_id=0, has_side_effects=True, vmem_limit_bytes=60 * 1024 * 1024
        ),
    )(
        query_proj,
        key_proj,
        value_proj,
        filter_taps,
        out_cotangent,
        *[jnp.asarray(entry) for entry in table],
    )
    return tuple(outs[at] for at in range(5))


def solution(mesh):
    placed = (P("ch", "seq"),) * 5
    return jax.shard_map(
        per_device, mesh=mesh, in_specs=placed, out_specs=placed, check_vma=False
    )
```

```python
import math

import jax
import jax.numpy as jnp
import numpy as np
from jax import lax
from jax.experimental import pallas as pl
from jax.experimental.pallas import tpu as pltpu
from jax.sharding import PartitionSpec as P

MESH = pl.DeviceIdType.MESH
LANES = 128
ROWS = 8
ITEMS = 3


def split_np(matrix):
    high = matrix.astype(jnp.bfloat16)
    low = (matrix - high.astype(np.float64)).astype(jnp.bfloat16)
    return high, low


def tables(run):
    k1 = np.arange(run)[:, None]
    n1 = np.arange(run)[None, :]
    first = ((2 * k1 + 1) * n1 % (4 * run)) * (2.0 * math.pi / (4 * run))
    first = np.concatenate([np.cos(first), -np.sin(first)], axis=0)
    n2 = np.arange(LANES)[None, :]
    turn = ((2 * k1 + 1) * n2) * (2.0 * math.pi / (4 * run * LANES))
    square = (np.arange(LANES)[:, None] * n2 % LANES) * (2.0 * math.pi / LANES)
    cos, sin = np.cos(square), np.sin(square)
    second = np.block([[cos, -sin], [sin, cos]])
    def left(matrix):
        high, low = split_np(matrix)
        return np.concatenate([high, high, low], axis=1)

    def right(matrix):
        high, low = split_np(matrix)
        return np.concatenate([high, high, low], axis=0)

    return (
        left(first),
        np.cos(turn).astype(np.float32),
        (-np.sin(turn)).astype(np.float32),
        right(second),
        right(second.T),
        left(first.T),
    )


def split(value):
    high = value.astype(jnp.bfloat16)
    low = (value - high.astype(jnp.float32)).astype(jnp.bfloat16)
    return high, low


def dot(left, right):
    return jnp.dot(left, right, preferred_element_type=jnp.float32)


def dot_left(table, value):
    high, low = split(value)
    return dot(table, jnp.concatenate([high, low, high], axis=0))


def dot_right(value, table):
    high, low = split(value)
    return dot(jnp.concatenate([high, low, high], axis=1), table)


def z_order(count):
    near = [step for half in range((count - 1) // 2, 0, -1) for step in (half, count - half)]
    return ([count // 2] if count % 2 == 0 else []) + near


def b_order(count):
    wide = count // 2
    steps = [(dx, dy) for dx in range(2) for dy in range(wide) if dx or dy]
    return sorted(steps, key=lambda step: -(step[0] + min(step[1], wide - step[1])))


def kernel(
    zs,
    bs,
    scale,
    q_hbm,
    k_hbm,
    v_hbm,
    f_hbm,
    o_hbm,
    *rest,
):
    table_hbm = rest[:6]
    out_ref = rest[6]
    (
        q_ref,
        k_ref,
        v_ref,
        f_ref,
        o_ref,
        *table_refs,
    ) = rest[7:18]
    (
        a_send,
        a_recv,
        b_send,
        b_recv,
        c_send,
        c_recv,
        d_send,
        d_recv,
        in_sem,
        send_sem,
        recv_sem,
    ) = rest[18:]
    run = zs * ROWS
    part = run // bs
    me = lax.axis_index("seq")
    block = me // zs
    lane = me % zs

    def z_peer(step):
        return lax.rem(lane + step, zs)

    def b_peer(step):
        wide = bs // 2
        across = lax.rem(lax.div(block, wide) + step[0], 2)
        return across * wide + lax.rem(lax.rem(block, wide) + step[1], wide)

    barrier = pltpu.get_barrier_semaphore()
    for step in z_order(zs):
        pl.semaphore_signal(
            barrier, inc=1, device_id={"seq": block * zs + z_peer(step)}, device_id_type=MESH
        )
    for step in b_order(bs):
        pl.semaphore_signal(
            barrier, inc=1, device_id={"seq": b_peer(step) * zs + lane}, device_id_type=MESH
        )

    loads = [
        pltpu.make_async_copy(src, dst, in_sem.at[at])
        for at, (src, dst) in enumerate(
            zip(
                (k_hbm, v_hbm, f_hbm, o_hbm, q_hbm) + tuple(table_hbm),
                (k_ref, v_ref, f_ref, o_ref, q_ref) + tuple(table_refs),
            )
        )
    ]
    for load in loads:
        load.start()

    def fill(item, value):
        for row in range(ROWS):
            a_send[:, item, row, :] = value[:, row * LANES : (row + 1) * LANES]
        a_recv[lane, item] = a_send[lane, item]

    def spread_z(phase, group, items, source, target):
        for step in z_order(zs):
            peer = z_peer(step)
            pltpu.make_async_remote_copy(
                src_ref=source.at[peer, items],
                dst_ref=target.at[lane, items],
                send_sem=send_sem.at[phase, group],
                recv_sem=recv_sem.at[phase, group],
                device_id={"seq": block * zs + peer},
                device_id_type=MESH,
            ).start()

    def await_z(sems, phase, group, items, buffer):
        whole = buffer.at[pl.ds(0, zs - 1), items]
        pltpu.make_async_copy(whole, whole, sems.at[phase, group]).wait()

    def spread_b(phase, item, source, target):
        for step in b_order(bs):
            peer = b_peer(step)
            pltpu.make_async_remote_copy(
                src_ref=source.at[item, peer],
                dst_ref=target.at[item, block],
                send_sem=send_sem.at[phase, item],
                recv_sem=recv_sem.at[phase, item],
                device_id={"seq": peer * zs + lane},
                device_id_type=MESH,
            ).start()

    def spread_c(group, items):
        for step in b_order(bs):
            peer = b_peer(step)
            pltpu.make_async_remote_copy(
                src_ref=c_send.at[peer, items],
                dst_ref=c_recv.at[block, items],
                send_sem=send_sem.at[2, group],
                recv_sem=recv_sem.at[2, group],
                device_id={"seq": peer * zs + lane},
                device_id_type=MESH,
            ).start()

    def await_c(sems, group, items, buffer):
        whole = buffer.at[pl.ds(0, bs - 1), items]
        pltpu.make_async_copy(whole, whole, sems.at[2, group]).wait()

    def await_all(sems, phase, item, buffer, count):
        whole = buffer.at[item, pl.ds(0, count - 1)]
        pltpu.make_async_copy(whole, whole, sems.at[phase, item]).wait()

    groups = (pl.ds(0, 2), pl.ds(2, 1))
    returns = (pl.ds(0, 1), pl.ds(1, 2))
    thirds = (pl.ds(0, 1), pl.ds(1, 1), pl.ds(2, 1))
    loads[0].wait()
    loads[1].wait()
    fill(0, k_ref[...] * v_ref[...])
    loads[2].wait()
    fill(1, f_ref[...])
    loads[3].wait()
    loads[4].wait()
    fill(2, o_ref[...] * q_ref[...])
    pl.semaphore_wait(barrier, zs - 1 + bs - 1)
    for group, items in enumerate(groups):
        spread_z(0, group, items, a_send, a_recv)
    for load in loads[5:]:
        load.wait()
    first, turn_real, turn_imag, second, second_back, first_back = table_refs

    def forward(items):
        rows = [a_recv[:, item].reshape(run, LANES) for item in items]
        sums = dot_left(first[...], jnp.concatenate(rows, axis=1))
        cos, sin = turn_real[...], turn_imag[...]
        turned = []
        for at in range(len(items)):
            here = slice(at * LANES, (at + 1) * LANES)
            real, imag = sums[:run, here], sums[run:, here]
            turned.append(
                jnp.concatenate([real * cos - imag * sin, real * sin + imag * cos], axis=1)
            )
        bins = dot_right(jnp.concatenate(turned, axis=0), second[...])
        for at, item in enumerate(items):
            here = slice(at * run, (at + 1) * run)
            b_send[item, :, 0] = bins[here, :LANES].reshape(bs, part, LANES)
            b_send[item, :, 1] = bins[here, LANES:].reshape(bs, part, LANES)
            b_recv[item, block] = b_send[item, block]
            spread_b(1, item, b_send, b_recv)

    sign = 1.0 - 2.0 * (lax.broadcasted_iota(jnp.int32, (part, LANES), 0) % 2).astype(jnp.float32)

    def spectrum(item, at):
        return b_recv[item, at, 0], b_recv[item, at, 1]

    def finish(item, sums, step, factor):
        for at in range(bs):
            real, imag = sums[at]
            other = at + step
            if 0 <= other < bs:
                over_real, over_imag = sums[other]
                real = real - factor * over_imag
                imag = imag + factor * over_real
            c_send[at, item, 0] = real
            c_send[at, item, 1] = imag
        c_recv[block, item] = c_send[block, item]

    def convolve(item, left, right):
        sums = []
        for at in range(bs):
            real = imag = None
            for of in range(at + 1):
                lr, li = spectrum(left, at - of)
                rr, ri = spectrum(right, of)
                pr, pi = lr * rr - li * ri, lr * ri + li * rr
                real, imag = (pr, pi) if real is None else (real + pr, imag + pi)
            sums.append((real, imag))
        finish(item, sums, -1, sign)

    def correlate(item, left, right):
        sums = []
        for at in range(bs):
            real = imag = None
            for of in range(bs - at):
                lr, li = spectrum(left, of)
                rr, ri = spectrum(right, at + of)
                pr, pi = lr * rr + li * ri, lr * ri - li * rr
                real, imag = (pr, pi) if real is None else (real + pr, imag + pi)
            sums.append((real, imag))
        finish(item, sums, 1, -sign)

    def inverse(items):
        bins = [
            jnp.concatenate(
                [c_recv[:, item, half].reshape(run, LANES) for half in range(2)], axis=1
            )
            for item in items
        ]
        sums = dot_right(jnp.concatenate(bins, axis=0), second_back[...])
        cos, sin = turn_real[...], turn_imag[...]
        turned = []
        for at in range(len(items)):
            here = slice(at * run, (at + 1) * run)
            real, imag = sums[here, :LANES], sums[here, LANES:]
            turned.append(
                jnp.concatenate([real * cos + imag * sin, imag * cos - real * sin], axis=0)
            )
        rows = dot_left(first_back[...], jnp.concatenate(turned, axis=1)) * scale
        for at, item in enumerate(items):
            here = slice(at * LANES, (at + 1) * LANES)
            d_send[:, item] = rows[:, here].reshape(zs, ROWS, LANES)
            d_recv[lane, item] = d_send[lane, item]

    await_z(recv_sem, 0, 0, groups[0], a_recv)
    forward((0, 1))
    await_z(recv_sem, 0, 1, groups[1], a_recv)
    forward((2,))
    await_all(recv_sem, 1, 0, b_recv, bs)
    await_all(recv_sem, 1, 1, b_recv, bs)
    convolve(0, 1, 0)
    spread_c(0, returns[0])
    await_all(recv_sem, 1, 2, b_recv, bs)
    correlate(1, 1, 2)
    spread_c(1, thirds[1])
    correlate(2, 0, 2)
    spread_c(2, thirds[2])
    await_c(recv_sem, 0, returns[0], c_recv)
    inverse((0,))
    spread_z(3, 0, returns[0], d_send, d_recv)
    await_c(recv_sem, 1, thirds[1], c_recv)
    await_c(recv_sem, 2, thirds[2], c_recv)
    inverse((1, 2))
    spread_z(3, 1, returns[1], d_send, d_recv)

    for item in range(ITEMS):
        await_all(send_sem, 1, item, b_send, bs)
    for group, items in enumerate(thirds):
        await_c(send_sem, group, items, c_send)
    for group, items in enumerate(groups):
        await_z(send_sem, 0, group, items, a_send)
    await_z(recv_sem, 3, 0, returns[0], d_recv)
    for row in range(ROWS):
        here = slice(row * LANES, (row + 1) * LANES)
        mixed = d_recv[:, 0, row, :]
        out_ref[0, :, here] = q_ref[:, here] * mixed
        out_ref[1, :, here] = o_ref[:, here] * mixed
    await_z(recv_sem, 3, 1, returns[1], d_recv)
    for row in range(ROWS):
        here = slice(row * LANES, (row + 1) * LANES)
        gated_grad = d_recv[:, 1, row, :]
        out_ref[2, :, here] = gated_grad * v_ref[:, here]
        out_ref[3, :, here] = gated_grad * k_ref[:, here]
    for row in range(ROWS):
        out_ref[4, :, row * LANES : (row + 1) * LANES] = d_recv[:, 2, row, :]
    for group, items in enumerate(returns):
        await_z(send_sem, 3, group, items, d_send)


def per_device(query_proj, key_proj, value_proj, filter_taps, out_cotangent):
    devices = lax.axis_size("seq")
    channels, tokens = filter_taps.shape
    zs = channels
    bs = devices // zs
    run = zs * ROWS
    part = run // bs
    scale = 1.0 / (run * LANES * math.sqrt(tokens * devices))
    table = tables(run)
    z_buffer = pltpu.VMEM((zs, ITEMS, ROWS, LANES), jnp.float32)
    c_buffer = pltpu.VMEM((bs, ITEMS, 2, part, LANES), jnp.float32)
    b_buffer = pltpu.VMEM((ITEMS, bs, 2, part, LANES), jnp.float32)
    body = lambda *refs: kernel(zs, bs, scale, *refs)
    outs = pl.pallas_call(
        body,
        out_shape=pltpu.VMEM((5, channels, tokens), jnp.float32),
        in_specs=[pl.BlockSpec(memory_space=pl.ANY)] * (5 + len(table)),
        out_specs=pl.BlockSpec(memory_space=pltpu.VMEM),
        scratch_shapes=[
            *[pltpu.VMEM((channels, tokens), jnp.float32) for _ in range(5)],
            *[pltpu.VMEM(entry.shape, entry.dtype) for entry in table],
            z_buffer,
            z_buffer,
            b_buffer,
            b_buffer,
            c_buffer,
            c_buffer,
            z_buffer,
            z_buffer,
            pltpu.SemaphoreType.DMA((5 + len(table),)),
            pltpu.SemaphoreType.DMA((4, ITEMS)),
            pltpu.SemaphoreType.DMA((4, ITEMS)),
        ],
        compiler_params=pltpu.CompilerParams(
            collective_id=0, has_side_effects=True, vmem_limit_bytes=60 * 1024 * 1024
        ),
    )(
        query_proj,
        key_proj,
        value_proj,
        filter_taps,
        out_cotangent,
        *[jnp.asarray(entry) for entry in table],
    )
    return tuple(outs[at] for at in range(5))


def solution(mesh):
    placed = (P("ch", "seq"),) * 5
    return jax.shard_map(
        per_device, mesh=mesh, in_specs=placed, out_specs=placed, check_vma=False
    )
```

```python
import math

import jax
import jax.numpy as jnp
import numpy as np
from jax import lax
from jax.experimental import pallas as pl
from jax.experimental.pallas import tpu as pltpu
from jax.sharding import PartitionSpec as P

MESH = pl.DeviceIdType.MESH
LANES = 128
ROWS = 8
ITEMS = 3


def split_np(matrix):
    high = matrix.astype(jnp.bfloat16)
    low = (matrix - high.astype(np.float64)).astype(jnp.bfloat16)
    return high, low


def tables(run):
    k1 = np.arange(run)[:, None]
    n1 = np.arange(run)[None, :]
    first = ((2 * k1 + 1) * n1 % (4 * run)) * (2.0 * math.pi / (4 * run))
    first = np.concatenate([np.cos(first), -np.sin(first)], axis=0)
    n2 = np.arange(LANES)[None, :]
    turn = ((2 * k1 + 1) * n2) * (2.0 * math.pi / (4 * run * LANES))
    square = (np.arange(LANES)[:, None] * n2 % LANES) * (2.0 * math.pi / LANES)
    cos, sin = np.cos(square), np.sin(square)
    second = np.block([[cos, -sin], [sin, cos]])
    def left(matrix):
        high, low = split_np(matrix)
        return np.concatenate([high, high, low], axis=1)

    def right(matrix):
        high, low = split_np(matrix)
        return np.concatenate([high, high, low], axis=0)

    return (
        left(first),
        np.cos(turn).astype(np.float32),
        (-np.sin(turn)).astype(np.float32),
        right(second),
        right(second.T),
        left(first.T),
    )


def split(value):
    high = value.astype(jnp.bfloat16)
    low = (value - high.astype(jnp.float32)).astype(jnp.bfloat16)
    return high, low


def dot(left, right):
    return jnp.dot(left, right, preferred_element_type=jnp.float32)


def dot_left(table, value):
    high, low = split(value)
    return dot(table, jnp.concatenate([high, low, high], axis=0))


def dot_right(value, table):
    high, low = split(value)
    return dot(jnp.concatenate([high, low, high], axis=1), table)


def z_order(count):
    near = [step for half in range((count - 1) // 2, 0, -1) for step in (half, count - half)]
    return ([count // 2] if count % 2 == 0 else []) + near


def b_order(count):
    wide = count // 2
    steps = [(dx, dy) for dx in range(2) for dy in range(wide) if dx or dy]
    return sorted(steps, key=lambda step: -(step[0] + min(step[1], wide - step[1])))


def kernel(
    zs,
    bs,
    scale,
    q_hbm,
    k_hbm,
    v_hbm,
    f_hbm,
    o_hbm,
    *rest,
):
    table_hbm = rest[:6]
    out_ref = rest[6]
    (
        q_ref,
        k_ref,
        v_ref,
        f_ref,
        o_ref,
        *table_refs,
    ) = rest[7:18]
    (
        a_send,
        a_recv,
        b_send,
        b_recv,
        c_send,
        c_recv,
        d_send,
        d_recv,
        in_sem,
        send_sem,
        recv_sem,
    ) = rest[18:]
    run = zs * ROWS
    part = run // bs
    me = lax.axis_index("seq")
    block = me // zs
    lane = me % zs

    def z_peer(step):
        return lax.rem(lane + step, zs)

    def b_peer(step):
        wide = bs // 2
        across = lax.rem(lax.div(block, wide) + step[0], 2)
        return across * wide + lax.rem(lax.rem(block, wide) + step[1], wide)

    barrier = pltpu.get_barrier_semaphore()
    for step in z_order(zs):
        pl.semaphore_signal(
            barrier, inc=1, device_id={"seq": block * zs + z_peer(step)}, device_id_type=MESH
        )
    for step in b_order(bs):
        pl.semaphore_signal(
            barrier, inc=1, device_id={"seq": b_peer(step) * zs + lane}, device_id_type=MESH
        )

    loads = [
        pltpu.make_async_copy(src, dst, in_sem.at[at])
        for at, (src, dst) in enumerate(
            zip(
                (k_hbm, v_hbm, f_hbm, o_hbm, q_hbm) + tuple(table_hbm),
                (k_ref, v_ref, f_ref, o_ref, q_ref) + tuple(table_refs),
            )
        )
    ]
    for load in loads:
        load.start()

    def fill(item, value):
        for row in range(ROWS):
            a_send[:, item, row, :] = value[:, row * LANES : (row + 1) * LANES]
        a_recv[lane, item] = a_send[lane, item]

    def spread_z(phase, group, items, source, target):
        for at, step in enumerate(z_order(zs)):
            peer = at + (lane <= at).astype(jnp.int32) if phase == 3 else z_peer(step)
            pltpu.make_async_remote_copy(
                src_ref=source.at[peer, items],
                dst_ref=target.at[lane, items],
                send_sem=send_sem.at[phase, group],
                recv_sem=recv_sem.at[phase, group],
                device_id={"seq": block * zs + peer},
                device_id_type=MESH,
            ).start()

    def await_z(sems, phase, group, items, buffer):
        whole = buffer.at[pl.ds(0, zs - 1), items]
        pltpu.make_async_copy(whole, whole, sems.at[phase, group]).wait()

    def spread_b(phase, item, source, target):
        for step in b_order(bs):
            peer = b_peer(step)
            pltpu.make_async_remote_copy(
                src_ref=source.at[item, peer],
                dst_ref=target.at[item, block],
                send_sem=send_sem.at[phase, item],
                recv_sem=recv_sem.at[phase, item],
                device_id={"seq": peer * zs + lane},
                device_id_type=MESH,
            ).start()

    def spread_c(group, items):
        for step in b_order(bs):
            peer = b_peer(step)
            pltpu.make_async_remote_copy(
                src_ref=c_send.at[peer, items],
                dst_ref=c_recv.at[block, items],
                send_sem=send_sem.at[2, group],
                recv_sem=recv_sem.at[2, group],
                device_id={"seq": peer * zs + lane},
                device_id_type=MESH,
            ).start()

    def await_c(sems, group, items, buffer):
        whole = buffer.at[pl.ds(0, bs - 1), items]
        pltpu.make_async_copy(whole, whole, sems.at[2, group]).wait()

    def await_all(sems, phase, item, buffer, count):
        whole = buffer.at[item, pl.ds(0, count - 1)]
        pltpu.make_async_copy(whole, whole, sems.at[phase, item]).wait()

    groups = (pl.ds(0, 2), pl.ds(2, 1))
    returns = (pl.ds(0, 1), pl.ds(1, 2))
    thirds = (pl.ds(0, 1), pl.ds(1, 1), pl.ds(2, 1))
    loads[0].wait()
    loads[1].wait()
    fill(0, k_ref[...] * v_ref[...])
    loads[2].wait()
    fill(1, f_ref[...])
    loads[3].wait()
    loads[4].wait()
    fill(2, o_ref[...] * q_ref[...])
    pl.semaphore_wait(barrier, zs - 1 + bs - 1)
    for group, items in enumerate(groups):
        spread_z(0, group, items, a_send, a_recv)
    for load in loads[5:]:
        load.wait()
    first, turn_real, turn_imag, second, second_back, first_back = table_refs

    def forward(items):
        rows = [a_recv[:, item].reshape(run, LANES) for item in items]
        sums = dot_left(first[...], jnp.concatenate(rows, axis=1))
        cos, sin = turn_real[...], turn_imag[...]
        turned = []
        for at in range(len(items)):
            here = slice(at * LANES, (at + 1) * LANES)
            real, imag = sums[:run, here], sums[run:, here]
            turned.append(
                jnp.concatenate([real * cos - imag * sin, real * sin + imag * cos], axis=1)
            )
        bins = dot_right(jnp.concatenate(turned, axis=0), second[...])
        for at, item in enumerate(items):
            here = slice(at * run, (at + 1) * run)
            b_send[item, :, 0] = bins[here, :LANES].reshape(bs, part, LANES)
            b_send[item, :, 1] = bins[here, LANES:].reshape(bs, part, LANES)
            b_recv[item, block] = b_send[item, block]
            spread_b(1, item, b_send, b_recv)

    sign = 1.0 - 2.0 * (lax.broadcasted_iota(jnp.int32, (part, LANES), 0) % 2).astype(jnp.float32)

    def spectrum(item, at):
        return b_recv[item, at, 0], b_recv[item, at, 1]

    def finish(item, sums, step, factor):
        for at in range(bs):
            real, imag = sums[at]
            other = at + step
            if 0 <= other < bs:
                over_real, over_imag = sums[other]
                real = real - factor * over_imag
                imag = imag + factor * over_real
            c_send[at, item, 0] = real
            c_send[at, item, 1] = imag
        c_recv[block, item] = c_send[block, item]

    def convolve(item, left, right):
        sums = []
        for at in range(bs):
            real = imag = None
            for of in range(at + 1):
                lr, li = spectrum(left, at - of)
                rr, ri = spectrum(right, of)
                pr, pi = lr * rr - li * ri, lr * ri + li * rr
                real, imag = (pr, pi) if real is None else (real + pr, imag + pi)
            sums.append((real, imag))
        finish(item, sums, -1, sign)

    def correlate(item, left, right):
        sums = []
        for at in range(bs):
            real = imag = None
            for of in range(bs - at):
                lr, li = spectrum(left, of)
                rr, ri = spectrum(right, at + of)
                pr, pi = lr * rr + li * ri, lr * ri - li * rr
                real, imag = (pr, pi) if real is None else (real + pr, imag + pi)
            sums.append((real, imag))
        finish(item, sums, 1, -sign)

    def inverse(items):
        bins = [
            jnp.concatenate(
                [c_recv[:, item, half].reshape(run, LANES) for half in range(2)], axis=1
            )
            for item in items
        ]
        sums = dot_right(jnp.concatenate(bins, axis=0), second_back[...])
        cos, sin = turn_real[...], turn_imag[...]
        turned = []
        for at in range(len(items)):
            here = slice(at * run, (at + 1) * run)
            real, imag = sums[here, :LANES], sums[here, LANES:]
            turned.append(
                jnp.concatenate([real * cos + imag * sin, imag * cos - real * sin], axis=0)
            )
        rows = dot_left(first_back[...], jnp.concatenate(turned, axis=1)) * scale
        for at, item in enumerate(items):
            here = slice(at * LANES, (at + 1) * LANES)
            d_send[:, item] = rows[:, here].reshape(zs, ROWS, LANES)
            d_recv[lane, item] = d_send[lane, item]

    await_z(recv_sem, 0, 0, groups[0], a_recv)
    forward((0, 1))
    await_z(recv_sem, 0, 1, groups[1], a_recv)
    forward((2,))
    await_all(recv_sem, 1, 0, b_recv, bs)
    await_all(recv_sem, 1, 1, b_recv, bs)
    convolve(0, 1, 0)
    spread_c(0, returns[0])
    await_all(recv_sem, 1, 2, b_recv, bs)
    correlate(1, 1, 2)
    spread_c(1, thirds[1])
    correlate(2, 0, 2)
    spread_c(2, thirds[2])
    await_c(recv_sem, 0, returns[0], c_recv)
    inverse((0,))
    spread_z(3, 0, returns[0], d_send, d_recv)
    await_c(recv_sem, 1, thirds[1], c_recv)
    await_c(recv_sem, 2, thirds[2], c_recv)
    inverse((1, 2))
    spread_z(3, 1, returns[1], d_send, d_recv)

    for item in range(ITEMS):
        await_all(send_sem, 1, item, b_send, bs)
    for group, items in enumerate(thirds):
        await_c(send_sem, group, items, c_send)
    for group, items in enumerate(groups):
        await_z(send_sem, 0, group, items, a_send)
    await_z(recv_sem, 3, 0, returns[0], d_recv)
    for row in range(ROWS):
        here = slice(row * LANES, (row + 1) * LANES)
        mixed = d_recv[:, 0, row, :]
        out_ref[0, :, here] = q_ref[:, here] * mixed
        out_ref[1, :, here] = o_ref[:, here] * mixed
    await_z(recv_sem, 3, 1, returns[1], d_recv)
    for row in range(ROWS):
        here = slice(row * LANES, (row + 1) * LANES)
        gated_grad = d_recv[:, 1, row, :]
        out_ref[2, :, here] = gated_grad * v_ref[:, here]
        out_ref[3, :, here] = gated_grad * k_ref[:, here]
    for row in range(ROWS):
        out_ref[4, :, row * LANES : (row + 1) * LANES] = d_recv[:, 2, row, :]
    for group, items in enumerate(returns):
        await_z(send_sem, 3, group, items, d_send)


def per_device(query_proj, key_proj, value_proj, filter_taps, out_cotangent):
    devices = lax.axis_size("seq")
    channels, tokens = filter_taps.shape
    zs = channels
    bs = devices // zs
    run = zs * ROWS
    part = run // bs
    scale = 1.0 / (run * LANES * math.sqrt(tokens * devices))
    table = tables(run)
    z_buffer = pltpu.VMEM((zs, ITEMS, ROWS, LANES), jnp.float32)
    c_buffer = pltpu.VMEM((bs, ITEMS, 2, part, LANES), jnp.float32)
    b_buffer = pltpu.VMEM((ITEMS, bs, 2, part, LANES), jnp.float32)
    body = lambda *refs: kernel(zs, bs, scale, *refs)
    outs = pl.pallas_call(
        body,
        out_shape=pltpu.VMEM((5, channels, tokens), jnp.float32),
        in_specs=[pl.BlockSpec(memory_space=pl.ANY)] * (5 + len(table)),
        out_specs=pl.BlockSpec(memory_space=pltpu.VMEM),
        scratch_shapes=[
            *[pltpu.VMEM((channels, tokens), jnp.float32) for _ in range(5)],
            *[pltpu.VMEM(entry.shape, entry.dtype) for entry in table],
            z_buffer,
            z_buffer,
            b_buffer,
            b_buffer,
            c_buffer,
            c_buffer,
            z_buffer,
            z_buffer,
            pltpu.SemaphoreType.DMA((5 + len(table),)),
            pltpu.SemaphoreType.DMA((4, ITEMS)),
            pltpu.SemaphoreType.DMA((4, ITEMS)),
        ],
        compiler_params=pltpu.CompilerParams(
            collective_id=0, has_side_effects=True, vmem_limit_bytes=60 * 1024 * 1024
        ),
    )(
        query_proj,
        key_proj,
        value_proj,
        filter_taps,
        out_cotangent,
        *[jnp.asarray(entry) for entry in table],
    )
    return tuple(outs[at] for at in range(5))


def solution(mesh):
    placed = (P("ch", "seq"),) * 5
    return jax.shard_map(
        per_device, mesh=mesh, in_specs=placed, out_specs=placed, check_vma=False
    )
```

```python
import math

import jax
import jax.numpy as jnp
import numpy as np
from jax import lax
from jax.experimental import pallas as pl
from jax.experimental.pallas import tpu as pltpu
from jax.sharding import PartitionSpec as P

MESH = pl.DeviceIdType.MESH
LANES = 128
ROWS = 8
ITEMS = 3


def split_np(matrix):
    high = matrix.astype(jnp.bfloat16)
    low = (matrix - high.astype(np.float64)).astype(jnp.bfloat16)
    return high, low


def tables(run):
    k1 = np.arange(run)[:, None]
    n1 = np.arange(run)[None, :]
    first = ((2 * k1 + 1) * n1 % (4 * run)) * (2.0 * math.pi / (4 * run))
    first = np.concatenate([np.cos(first), -np.sin(first)], axis=0)
    n2 = np.arange(LANES)[None, :]
    turn = ((2 * k1 + 1) * n2) * (2.0 * math.pi / (4 * run * LANES))
    square = (np.arange(LANES)[:, None] * n2 % LANES) * (2.0 * math.pi / LANES)
    cos, sin = np.cos(square), np.sin(square)
    second = np.block([[cos, -sin], [sin, cos]])
    def left(matrix):
        high, low = split_np(matrix)
        return np.concatenate([high, high, low], axis=1)

    def right(matrix):
        high, low = split_np(matrix)
        return np.concatenate([high, high, low], axis=0)

    return (
        left(first),
        np.cos(turn).astype(np.float32),
        (-np.sin(turn)).astype(np.float32),
        right(second),
        right(second.T),
        left(first.T),
    )


def split(value):
    high = value.astype(jnp.bfloat16)
    low = (value - high.astype(jnp.float32)).astype(jnp.bfloat16)
    return high, low


def dot(left, right):
    return jnp.dot(left, right, preferred_element_type=jnp.float32)


def dot_left(table, value):
    high, low = split(value)
    return dot(table, jnp.concatenate([high, low, high], axis=0))


def dot_right(value, table):
    high, low = split(value)
    return dot(jnp.concatenate([high, low, high], axis=1), table)


def z_order(count):
    near = [step for half in range((count - 1) // 2, 0, -1) for step in (half, count - half)]
    return ([count // 2] if count % 2 == 0 else []) + near


def b_order(count):
    wide = count // 2
    steps = [(dx, dy) for dx in range(2) for dy in range(wide) if dx or dy]
    return sorted(steps, key=lambda step: -(step[0] + min(step[1], wide - step[1])))


def kernel(
    zs,
    bs,
    scale,
    q_hbm,
    k_hbm,
    v_hbm,
    f_hbm,
    o_hbm,
    *rest,
):
    table_hbm = rest[:6]
    out_ref = rest[6]
    (
        q_ref,
        k_ref,
        v_ref,
        f_ref,
        o_ref,
        *table_refs,
    ) = rest[7:18]
    (
        a_send,
        a_recv,
        b_send,
        b_recv,
        c_send,
        c_recv,
        d_send,
        d_recv,
        in_sem,
        send_sem,
        recv_sem,
    ) = rest[18:]
    run = zs * ROWS
    part = run // bs
    me = lax.axis_index("seq")
    block = me // zs
    lane = me % zs

    def z_peer(step):
        return lax.rem(lane + step, zs)

    def b_peer(step):
        wide = bs // 2
        across = lax.rem(lax.div(block, wide) + step[0], 2)
        return across * wide + lax.rem(lax.rem(block, wide) + step[1], wide)

    barrier = pltpu.get_barrier_semaphore()
    for step in z_order(zs):
        pl.semaphore_signal(
            barrier, inc=1, device_id={"seq": block * zs + z_peer(step)}, device_id_type=MESH
        )
    for step in b_order(bs):
        pl.semaphore_signal(
            barrier, inc=1, device_id={"seq": b_peer(step) * zs + lane}, device_id_type=MESH
        )

    loads = [
        pltpu.make_async_copy(src, dst, in_sem.at[at])
        for at, (src, dst) in enumerate(
            zip(
                (k_hbm, v_hbm, f_hbm, o_hbm, q_hbm) + tuple(table_hbm),
                (k_ref, v_ref, f_ref, o_ref, q_ref) + tuple(table_refs),
            )
        )
    ]
    for load in loads:
        load.start()

    def fill(item, value):
        for row in range(ROWS):
            a_send[:, item, row, :] = value[:, row * LANES : (row + 1) * LANES]
        a_recv[lane, item] = a_send[lane, item]

    def spread_z(phase, group, items, source, target):
        for at, step in enumerate(z_order(zs)):
            peer = at + (lane <= at).astype(jnp.int32) if phase == 3 else z_peer(step)
            pltpu.make_async_remote_copy(
                src_ref=source.at[peer, items],
                dst_ref=target.at[lane, items],
                send_sem=send_sem.at[phase, group],
                recv_sem=recv_sem.at[phase, group],
                device_id={"seq": block * zs + peer},
                device_id_type=MESH,
            ).start()

    def await_z(sems, phase, group, items, buffer):
        whole = buffer.at[pl.ds(0, zs - 1), items]
        pltpu.make_async_copy(whole, whole, sems.at[phase, group]).wait()

    def spread_b(phase, group, items, source, target):
        for step in b_order(bs):
            peer = b_peer(step)
            pltpu.make_async_remote_copy(
                src_ref=source.at[peer, items],
                dst_ref=target.at[block, items],
                send_sem=send_sem.at[phase, group],
                recv_sem=recv_sem.at[phase, group],
                device_id={"seq": peer * zs + lane},
                device_id_type=MESH,
            ).start()

    def await_b(sems, phase, group, items, buffer):
        whole = buffer.at[pl.ds(0, bs - 1), items]
        pltpu.make_async_copy(whole, whole, sems.at[phase, group]).wait()

    groups = (pl.ds(0, 2), pl.ds(2, 1))
    returns = (pl.ds(0, 1), pl.ds(1, 2))
    thirds = (pl.ds(0, 1), pl.ds(1, 1), pl.ds(2, 1))
    loads[0].wait()
    loads[1].wait()
    fill(0, k_ref[...] * v_ref[...])
    loads[2].wait()
    fill(1, f_ref[...])
    loads[3].wait()
    loads[4].wait()
    fill(2, o_ref[...] * q_ref[...])
    pl.semaphore_wait(barrier, zs - 1 + bs - 1)
    for group, items in enumerate(groups):
        spread_z(0, group, items, a_send, a_recv)
    for load in loads[5:]:
        load.wait()
    first, turn_real, turn_imag, second, second_back, first_back = table_refs

    def forward(items):
        rows = [a_recv[:, item].reshape(run, LANES) for item in items]
        sums = dot_left(first[...], jnp.concatenate(rows, axis=1))
        cos, sin = turn_real[...], turn_imag[...]
        turned = []
        for at in range(len(items)):
            here = slice(at * LANES, (at + 1) * LANES)
            real, imag = sums[:run, here], sums[run:, here]
            turned.append(
                jnp.concatenate([real * cos - imag * sin, real * sin + imag * cos], axis=1)
            )
        bins = dot_right(jnp.concatenate(turned, axis=0), second[...])
        for at, item in enumerate(items):
            here = slice(at * run, (at + 1) * run)
            b_send[:, item, 0] = bins[here, :LANES].reshape(bs, part, LANES)
            b_send[:, item, 1] = bins[here, LANES:].reshape(bs, part, LANES)
            b_recv[block, item] = b_send[block, item]

    sign = 1.0 - 2.0 * (lax.broadcasted_iota(jnp.int32, (part, LANES), 0) % 2).astype(jnp.float32)

    def spectrum(item, at):
        return b_recv[at, item, 0], b_recv[at, item, 1]

    def finish(item, sums, step, factor):
        for at in range(bs):
            real, imag = sums[at]
            other = at + step
            if 0 <= other < bs:
                over_real, over_imag = sums[other]
                real = real - factor * over_imag
                imag = imag + factor * over_real
            c_send[at, item, 0] = real
            c_send[at, item, 1] = imag
        c_recv[block, item] = c_send[block, item]

    def convolve(item, left, right):
        sums = []
        for at in range(bs):
            real = imag = None
            for of in range(at + 1):
                lr, li = spectrum(left, at - of)
                rr, ri = spectrum(right, of)
                pr, pi = lr * rr - li * ri, lr * ri + li * rr
                real, imag = (pr, pi) if real is None else (real + pr, imag + pi)
            sums.append((real, imag))
        finish(item, sums, -1, sign)

    def correlate(item, left, right):
        sums = []
        for at in range(bs):
            real = imag = None
            for of in range(bs - at):
                lr, li = spectrum(left, of)
                rr, ri = spectrum(right, at + of)
                pr, pi = lr * rr + li * ri, lr * ri - li * rr
                real, imag = (pr, pi) if real is None else (real + pr, imag + pi)
            sums.append((real, imag))
        finish(item, sums, 1, -sign)

    def inverse(items):
        bins = [
            jnp.concatenate(
                [c_recv[:, item, half].reshape(run, LANES) for half in range(2)], axis=1
            )
            for item in items
        ]
        sums = dot_right(jnp.concatenate(bins, axis=0), second_back[...])
        cos, sin = turn_real[...], turn_imag[...]
        turned = []
        for at in range(len(items)):
            here = slice(at * run, (at + 1) * run)
            real, imag = sums[here, :LANES], sums[here, LANES:]
            turned.append(
                jnp.concatenate([real * cos + imag * sin, imag * cos - real * sin], axis=0)
            )
        rows = dot_left(first_back[...], jnp.concatenate(turned, axis=1)) * scale
        for at, item in enumerate(items):
            here = slice(at * LANES, (at + 1) * LANES)
            d_send[:, item] = rows[:, here].reshape(zs, ROWS, LANES)
            d_recv[lane, item] = d_send[lane, item]

    await_z(recv_sem, 0, 0, groups[0], a_recv)
    forward((0, 1))
    spread_b(1, 0, groups[0], b_send, b_recv)
    await_z(recv_sem, 0, 1, groups[1], a_recv)
    forward((2,))
    spread_b(1, 1, groups[1], b_send, b_recv)
    await_b(recv_sem, 1, 0, groups[0], b_recv)
    convolve(0, 1, 0)
    spread_b(2, 0, returns[0], c_send, c_recv)
    await_b(recv_sem, 1, 1, groups[1], b_recv)
    correlate(1, 1, 2)
    spread_b(2, 1, thirds[1], c_send, c_recv)
    correlate(2, 0, 2)
    spread_b(2, 2, thirds[2], c_send, c_recv)
    await_b(recv_sem, 2, 0, returns[0], c_recv)
    inverse((0,))
    spread_z(3, 0, returns[0], d_send, d_recv)
    await_b(recv_sem, 2, 1, thirds[1], c_recv)
    await_b(recv_sem, 2, 2, thirds[2], c_recv)
    inverse((1, 2))
    spread_z(3, 1, returns[1], d_send, d_recv)

    for group, items in enumerate(groups):
        await_b(send_sem, 1, group, items, b_send)
    for group, items in enumerate(thirds):
        await_b(send_sem, 2, group, items, c_send)
    for group, items in enumerate(groups):
        await_z(send_sem, 0, group, items, a_send)
    await_z(recv_sem, 3, 0, returns[0], d_recv)
    for row in range(ROWS):
        here = slice(row * LANES, (row + 1) * LANES)
        mixed = d_recv[:, 0, row, :]
        out_ref[0, :, here] = q_ref[:, here] * mixed
        out_ref[1, :, here] = o_ref[:, here] * mixed
    await_z(recv_sem, 3, 1, returns[1], d_recv)
    for row in range(ROWS):
        here = slice(row * LANES, (row + 1) * LANES)
        gated_grad = d_recv[:, 1, row, :]
        out_ref[2, :, here] = gated_grad * v_ref[:, here]
        out_ref[3, :, here] = gated_grad * k_ref[:, here]
    for row in range(ROWS):
        out_ref[4, :, row * LANES : (row + 1) * LANES] = d_recv[:, 2, row, :]
    for group, items in enumerate(returns):
        await_z(send_sem, 3, group, items, d_send)


def per_device(query_proj, key_proj, value_proj, filter_taps, out_cotangent):
    devices = lax.axis_size("seq")
    channels, tokens = filter_taps.shape
    zs = channels
    bs = devices // zs
    run = zs * ROWS
    part = run // bs
    scale = 1.0 / (run * LANES * math.sqrt(tokens * devices))
    table = tables(run)
    z_buffer = pltpu.VMEM((zs, ITEMS, ROWS, LANES), jnp.float32)
    b_buffer = pltpu.VMEM((bs, ITEMS, 2, part, LANES), jnp.float32)
    body = lambda *refs: kernel(zs, bs, scale, *refs)
    outs = pl.pallas_call(
        body,
        out_shape=pltpu.VMEM((5, channels, tokens), jnp.float32),
        in_specs=[pl.BlockSpec(memory_space=pl.ANY)] * (5 + len(table)),
        out_specs=pl.BlockSpec(memory_space=pltpu.VMEM),
        scratch_shapes=[
            *[pltpu.VMEM((channels, tokens), jnp.float32) for _ in range(5)],
            *[pltpu.VMEM(entry.shape, entry.dtype) for entry in table],
            z_buffer,
            z_buffer,
            b_buffer,
            b_buffer,
            b_buffer,
            b_buffer,
            z_buffer,
            z_buffer,
            pltpu.SemaphoreType.DMA((5 + len(table),)),
            pltpu.SemaphoreType.DMA((4, ITEMS)),
            pltpu.SemaphoreType.DMA((4, ITEMS)),
        ],
        compiler_params=pltpu.CompilerParams(
            collective_id=0, has_side_effects=True, vmem_limit_bytes=60 * 1024 * 1024
        ),
    )(
        query_proj,
        key_proj,
        value_proj,
        filter_taps,
        out_cotangent,
        *[jnp.asarray(entry) for entry in table],
    )
    return tuple(outs[at] for at in range(5))


def solution(mesh):
    placed = (P("ch", "seq"),) * 5
    return jax.shard_map(
        per_device, mesh=mesh, in_specs=placed, out_specs=placed, check_vma=False
    )
```

```python
import math

import jax
import jax.numpy as jnp
import numpy as np
from jax import lax
from jax.experimental import pallas as pl
from jax.experimental.pallas import tpu as pltpu
from jax.sharding import PartitionSpec as P

MESH = pl.DeviceIdType.MESH
LANES = 128
ROWS = 8
ITEMS = 3


def split_np(matrix):
    high = matrix.astype(jnp.bfloat16)
    low = (matrix - high.astype(np.float64)).astype(jnp.bfloat16)
    return high, low


def tables(run):
    k1 = np.arange(run)[:, None]
    n1 = np.arange(run)[None, :]
    first = ((2 * k1 + 1) * n1 % (4 * run)) * (2.0 * math.pi / (4 * run))
    first = np.concatenate([np.cos(first), -np.sin(first)], axis=0)
    n2 = np.arange(LANES)[None, :]
    turn = ((2 * k1 + 1) * n2) * (2.0 * math.pi / (4 * run * LANES))
    square = (np.arange(LANES)[:, None] * n2 % LANES) * (2.0 * math.pi / LANES)
    cos, sin = np.cos(square), np.sin(square)
    second = np.block([[cos, -sin], [sin, cos]])
    def left(matrix):
        high, low = split_np(matrix)
        return np.concatenate([high, high, low], axis=1)

    def right(matrix):
        high, low = split_np(matrix)
        return np.concatenate([high, high, low], axis=0)

    return (
        left(first),
        np.cos(turn).astype(np.float32),
        (-np.sin(turn)).astype(np.float32),
        right(second),
        right(second.T),
        left(first.T),
    )


def split(value):
    high = value.astype(jnp.bfloat16)
    low = (value - high.astype(jnp.float32)).astype(jnp.bfloat16)
    return high, low


def dot(left, right):
    return jnp.dot(left, right, preferred_element_type=jnp.float32)


def dot_left(table, value):
    high, low = split(value)
    return dot(table, jnp.concatenate([high, low, high], axis=0))


def dot_right(value, table):
    high, low = split(value)
    return dot(jnp.concatenate([high, low, high], axis=1), table)


def z_order(count):
    near = [step for half in range((count - 1) // 2, 0, -1) for step in (half, count - half)]
    return ([count // 2] if count % 2 == 0 else []) + near


def b_order(count):
    wide = count // 2
    steps = [(dx, dy) for dx in range(2) for dy in range(wide) if dx or dy]
    return sorted(steps, key=lambda step: -(step[0] + min(step[1], wide - step[1])))


def kernel(
    zs,
    bs,
    scale,
    q_hbm,
    k_hbm,
    v_hbm,
    f_hbm,
    o_hbm,
    *rest,
):
    table_hbm = rest[:6]
    out_ref = rest[6]
    (
        q_ref,
        k_ref,
        v_ref,
        f_ref,
        o_ref,
        *table_refs,
    ) = rest[7:18]
    (
        a_send,
        a_recv,
        b_send,
        b_recv,
        c_send,
        c_recv,
        d_send,
        d_recv,
        in_sem,
        send_sem,
        recv_sem,
    ) = rest[18:]
    run = zs * ROWS
    part = run // bs
    me = lax.axis_index("seq")
    block = me // zs
    lane = me % zs

    def z_peer(step):
        return lax.rem(lane + step, zs)

    def b_peer(step):
        wide = bs // 2
        across = lax.rem(lax.div(block, wide) + step[0], 2)
        return across * wide + lax.rem(lax.rem(block, wide) + step[1], wide)

    barrier = pltpu.get_barrier_semaphore()
    for step in z_order(zs):
        pl.semaphore_signal(
            barrier, inc=1, device_id={"seq": block * zs + z_peer(step)}, device_id_type=MESH
        )
    for step in b_order(bs):
        pl.semaphore_signal(
            barrier, inc=1, device_id={"seq": b_peer(step) * zs + lane}, device_id_type=MESH
        )

    loads = [
        pltpu.make_async_copy(src, dst, in_sem.at[at])
        for at, (src, dst) in enumerate(
            zip(
                (k_hbm, v_hbm, f_hbm, o_hbm, q_hbm) + tuple(table_hbm),
                (k_ref, v_ref, f_ref, o_ref, q_ref) + tuple(table_refs),
            )
        )
    ]
    for load in loads:
        load.start()

    def fill(item, value):
        for row in range(ROWS):
            a_send[:, item, row, :] = value[:, row * LANES : (row + 1) * LANES]
        a_recv[lane, item] = a_send[lane, item]

    def spread_z(phase, group, items, source, target):
        for at, step in enumerate(z_order(zs)):
            last = phase == 3 and group == 1
            peer = at + (lane <= at).astype(jnp.int32) if last else z_peer(step)
            pltpu.make_async_remote_copy(
                src_ref=source.at[peer, items],
                dst_ref=target.at[lane, items],
                send_sem=send_sem.at[phase, group],
                recv_sem=recv_sem.at[phase, group],
                device_id={"seq": block * zs + peer},
                device_id_type=MESH,
            ).start()

    def await_z(sems, phase, group, items, buffer):
        whole = buffer.at[pl.ds(0, zs - 1), items]
        pltpu.make_async_copy(whole, whole, sems.at[phase, group]).wait()

    def spread_b(phase, item, source, target):
        for step in b_order(bs):
            peer = b_peer(step)
            pltpu.make_async_remote_copy(
                src_ref=source.at[item, peer],
                dst_ref=target.at[item, block],
                send_sem=send_sem.at[phase, item],
                recv_sem=recv_sem.at[phase, item],
                device_id={"seq": peer * zs + lane},
                device_id_type=MESH,
            ).start()

    def spread_c(group, items):
        for step in b_order(bs):
            peer = b_peer(step)
            pltpu.make_async_remote_copy(
                src_ref=c_send.at[peer, items],
                dst_ref=c_recv.at[block, items],
                send_sem=send_sem.at[2, group],
                recv_sem=recv_sem.at[2, group],
                device_id={"seq": peer * zs + lane},
                device_id_type=MESH,
            ).start()

    def await_c(sems, group, items, buffer):
        whole = buffer.at[pl.ds(0, bs - 1), items]
        pltpu.make_async_copy(whole, whole, sems.at[2, group]).wait()

    def await_all(sems, phase, item, buffer, count):
        whole = buffer.at[item, pl.ds(0, count - 1)]
        pltpu.make_async_copy(whole, whole, sems.at[phase, item]).wait()

    groups = (pl.ds(0, 2), pl.ds(2, 1))
    returns = (pl.ds(0, 1), pl.ds(1, 2))
    thirds = (pl.ds(0, 1), pl.ds(1, 1), pl.ds(2, 1))
    loads[0].wait()
    loads[1].wait()
    fill(0, k_ref[...] * v_ref[...])
    loads[2].wait()
    fill(1, f_ref[...])
    loads[3].wait()
    loads[4].wait()
    fill(2, o_ref[...] * q_ref[...])
    pl.semaphore_wait(barrier, zs - 1 + bs - 1)
    for group, items in enumerate(groups):
        spread_z(0, group, items, a_send, a_recv)
    for load in loads[5:]:
        load.wait()
    first, turn_real, turn_imag, second, second_back, first_back = table_refs

    def forward(items):
        rows = [a_recv[:, item].reshape(run, LANES) for item in items]
        sums = dot_left(first[...], jnp.concatenate(rows, axis=1))
        cos, sin = turn_real[...], turn_imag[...]
        turned = []
        for at in range(len(items)):
            here = slice(at * LANES, (at + 1) * LANES)
            real, imag = sums[:run, here], sums[run:, here]
            turned.append(
                jnp.concatenate([real * cos - imag * sin, real * sin + imag * cos], axis=1)
            )
        bins = dot_right(jnp.concatenate(turned, axis=0), second[...])
        for at, item in enumerate(items):
            here = slice(at * run, (at + 1) * run)
            b_send[item, :, 0] = bins[here, :LANES].reshape(bs, part, LANES)
            b_send[item, :, 1] = bins[here, LANES:].reshape(bs, part, LANES)
            b_recv[item, block] = b_send[item, block]
            spread_b(1, item, b_send, b_recv)

    sign = 1.0 - 2.0 * (lax.broadcasted_iota(jnp.int32, (part, LANES), 0) % 2).astype(jnp.float32)

    def spectrum(item, at):
        return b_recv[item, at, 0], b_recv[item, at, 1]

    def finish(item, sums, step, factor):
        for at in range(bs):
            real, imag = sums[at]
            other = at + step
            if 0 <= other < bs:
                over_real, over_imag = sums[other]
                real = real - factor * over_imag
                imag = imag + factor * over_real
            c_send[at, item, 0] = real
            c_send[at, item, 1] = imag
        c_recv[block, item] = c_send[block, item]

    def convolve(item, left, right):
        sums = []
        for at in range(bs):
            real = imag = None
            for of in range(at + 1):
                lr, li = spectrum(left, at - of)
                rr, ri = spectrum(right, of)
                pr, pi = lr * rr - li * ri, lr * ri + li * rr
                real, imag = (pr, pi) if real is None else (real + pr, imag + pi)
            sums.append((real, imag))
        finish(item, sums, -1, sign)

    def correlate(item, left, right):
        sums = []
        for at in range(bs):
            real = imag = None
            for of in range(bs - at):
                lr, li = spectrum(left, of)
                rr, ri = spectrum(right, at + of)
                pr, pi = lr * rr + li * ri, lr * ri - li * rr
                real, imag = (pr, pi) if real is None else (real + pr, imag + pi)
            sums.append((real, imag))
        finish(item, sums, 1, -sign)

    def inverse(items):
        bins = [
            jnp.concatenate(
                [c_recv[:, item, half].reshape(run, LANES) for half in range(2)], axis=1
            )
            for item in items
        ]
        sums = dot_right(jnp.concatenate(bins, axis=0), second_back[...])
        cos, sin = turn_real[...], turn_imag[...]
        turned = []
        for at in range(len(items)):
            here = slice(at * run, (at + 1) * run)
            real, imag = sums[here, :LANES], sums[here, LANES:]
            turned.append(
                jnp.concatenate([real * cos + imag * sin, imag * cos - real * sin], axis=0)
            )
        rows = dot_left(first_back[...], jnp.concatenate(turned, axis=1)) * scale
        for at, item in enumerate(items):
            here = slice(at * LANES, (at + 1) * LANES)
            d_send[:, item] = rows[:, here].reshape(zs, ROWS, LANES)
            d_recv[lane, item] = d_send[lane, item]

    await_z(recv_sem, 0, 0, groups[0], a_recv)
    forward((0, 1))
    await_z(recv_sem, 0, 1, groups[1], a_recv)
    forward((2,))
    await_all(recv_sem, 1, 0, b_recv, bs)
    await_all(recv_sem, 1, 1, b_recv, bs)
    convolve(0, 1, 0)
    spread_c(0, returns[0])
    await_all(recv_sem, 1, 2, b_recv, bs)
    correlate(1, 1, 2)
    spread_c(1, thirds[1])
    correlate(2, 0, 2)
    spread_c(2, thirds[2])
    await_c(recv_sem, 0, returns[0], c_recv)
    inverse((0,))
    spread_z(3, 0, returns[0], d_send, d_recv)
    await_c(recv_sem, 1, thirds[1], c_recv)
    await_c(recv_sem, 2, thirds[2], c_recv)
    inverse((1, 2))
    spread_z(3, 1, returns[1], d_send, d_recv)

    for item in range(ITEMS):
        await_all(send_sem, 1, item, b_send, bs)
    for group, items in enumerate(thirds):
        await_c(send_sem, group, items, c_send)
    for group, items in enumerate(groups):
        await_z(send_sem, 0, group, items, a_send)
    await_z(recv_sem, 3, 0, returns[0], d_recv)
    for row in range(ROWS):
        here = slice(row * LANES, (row + 1) * LANES)
        mixed = d_recv[:, 0, row, :]
        out_ref[0, :, here] = q_ref[:, here] * mixed
        out_ref[1, :, here] = o_ref[:, here] * mixed
    await_z(recv_sem, 3, 1, returns[1], d_recv)
    for row in range(ROWS):
        here = slice(row * LANES, (row + 1) * LANES)
        gated_grad = d_recv[:, 1, row, :]
        out_ref[2, :, here] = gated_grad * v_ref[:, here]
        out_ref[3, :, here] = gated_grad * k_ref[:, here]
    for row in range(ROWS):
        out_ref[4, :, row * LANES : (row + 1) * LANES] = d_recv[:, 2, row, :]
    for group, items in enumerate(returns):
        await_z(send_sem, 3, group, items, d_send)


def per_device(query_proj, key_proj, value_proj, filter_taps, out_cotangent):
    devices = lax.axis_size("seq")
    channels, tokens = filter_taps.shape
    zs = channels
    bs = devices // zs
    run = zs * ROWS
    part = run // bs
    scale = 1.0 / (run * LANES * math.sqrt(tokens * devices))
    table = tables(run)
    z_buffer = pltpu.VMEM((zs, ITEMS, ROWS, LANES), jnp.float32)
    c_buffer = pltpu.VMEM((bs, ITEMS, 2, part, LANES), jnp.float32)
    b_buffer = pltpu.VMEM((ITEMS, bs, 2, part, LANES), jnp.float32)
    body = lambda *refs: kernel(zs, bs, scale, *refs)
    outs = pl.pallas_call(
        body,
        out_shape=pltpu.VMEM((5, channels, tokens), jnp.float32),
        in_specs=[pl.BlockSpec(memory_space=pl.ANY)] * (5 + len(table)),
        out_specs=pl.BlockSpec(memory_space=pltpu.VMEM),
        scratch_shapes=[
            *[pltpu.VMEM((channels, tokens), jnp.float32) for _ in range(5)],
            *[pltpu.VMEM(entry.shape, entry.dtype) for entry in table],
            z_buffer,
            z_buffer,
            b_buffer,
            b_buffer,
            c_buffer,
            c_buffer,
            z_buffer,
            z_buffer,
            pltpu.SemaphoreType.DMA((5 + len(table),)),
            pltpu.SemaphoreType.DMA((4, ITEMS)),
            pltpu.SemaphoreType.DMA((4, ITEMS)),
        ],
        compiler_params=pltpu.CompilerParams(
            collective_id=0, has_side_effects=True, vmem_limit_bytes=60 * 1024 * 1024
        ),
    )(
        query_proj,
        key_proj,
        value_proj,
        filter_taps,
        out_cotangent,
        *[jnp.asarray(entry) for entry in table],
    )
    return tuple(outs[at] for at in range(5))


def solution(mesh):
    placed = (P("ch", "seq"),) * 5
    return jax.shard_map(
        per_device, mesh=mesh, in_specs=placed, out_specs=placed, check_vma=False
    )
```
